32 devices in a mesh: region: 8 (over z, y), chan: 4 (over x, core).
Axes of the slice: x: 2, y: 2, z: 4, core: 2. Of those that a mesh axis runs over, the one named last changes fastest.
Arguments:
- grid_state: bfloat16 [8192, 1024], P('region', 'chan'), may hold values from -6 to 6
- mesh_state: bfloat16 [2048, 1024], P('region', 'chan'), may hold values from -6 to 6
- enc_send: bfloat16 [1024, 1024], P(None, 'chan'), may hold values from -0.1875 to 0.1875
- enc_out: bfloat16 [1024, 1024], P(None, 'chan'), may hold values from -0.1875 to 0.1875
- proc_send: bfloat16 [1024, 1024], P(None, 'chan'), may hold values from -0.1875 to 0.1875
- proc_out: bfloat16 [1024, 1024], P(None, 'chan'), may hold values from -0.1875 to 0.1875
- dec_send: bfloat16 [1024, 1024], P(None, 'chan'), may hold values from -0.1875 to 0.1875
- dec_out: bfloat16 [1024, 1024], P(None, 'chan'), may hold values from -0.1875 to 0.1875
- g2m_index: int32 [16, 2048], P(None, 'region'), may hold values from 0 to 8191, as said below
- g2m_weight: float32 [16, 2048], P(None, 'region'), may hold values from 0.25 to 4
- g2m_count: int32 [2048], P('region'), may hold values from 1 to 16
- m2m_index: int32 [8, 2048], P(None, 'region'), may hold values from 0 to 2047, as said below
- m2m_weight: float32 [8, 2048], P(None, 'region'), may hold values from 0.25 to 4
- m2m_count: int32 [2048], P('region'), may hold values from 1 to 8
- m2g_index: int32 [4, 8192], P(None, 'region'), may hold values from 0 to 2047, as said below
- m2g_weight: float32 [4, 8192], P(None, 'region'), may hold values from 0.25 to 4
- m2g_count: int32 [8192], P('region'), may hold values from 1 to 4
Outputs:
- grid_next: bfloat16 [8192, 1024], P('region', 'chan')
- mesh_next: bfloat16 [2048, 1024], P('region', 'chan')
The draws below stay inside these ranges and needn't reach their ends.
Inputs may be any that keep to these rules, and one draw needn't show every extreme that they name: Column i of g2m_index belongs to mesh node i, of region i // 256; each entry names a grid node whose region (index // 1024) differs from it by at most 2. `m2m_index`: column i belongs to mesh node i, of region i // 256; each entry names a mesh node whose region (index // 256) differs from it by at most 2. `m2g_index`: column i belongs to grid node i, of region i // 1024; each entry names a mesh node whose region (index // 256) differs from it by at most 2.
All inputs are finite; a program needn't handle non-finite values.
Results may differ from the reference program's by a relative error of at most 0.017.
Values may be sent and summed in bfloat16 or wider, within the bound.
A program may use at most 64 MiB of HBM per device.

```python
import math
import jax
import jax.numpy as jnp
from jax import lax

H = 1024
G_DEV = 1024
M_DEV = 256
K_E = 16
K_M = 8
K_D = 4
SPAN = 2
GRID = 8192
MESH = 2048
N_REGION = 8


def neighbours(key, fanin, recv_dev, send_dev, recv_total):
    regions = recv_total // recv_dev
    column = jnp.arange(recv_total, dtype=jnp.int32) // recv_dev
    key_offset, key_row = jax.random.split(key)
    offset = jax.random.randint(key_offset, (fanin, recv_total), -SPAN, SPAN + 1, dtype=jnp.int32)
    block = jnp.clip(column[None, :] + offset, 0, regions - 1)
    row_pick = jax.random.randint(key_row, (fanin, recv_total), 0, send_dev, dtype=jnp.int32)
    return (block * send_dev + row_pick).astype(jnp.int32)


def draw_g2m_index(key, part):
    key = jax.random.fold_in(key, 11)
    return neighbours(key, K_E, M_DEV, G_DEV, MESH)


def draw_m2m_index(key, part):
    key = jax.random.fold_in(key, 12)
    return neighbours(key, K_M, M_DEV, M_DEV, MESH)


def draw_m2g_index(key, part):
    key = jax.random.fold_in(key, 13)
    return neighbours(key, K_D, G_DEV, M_DEV, GRID)


def place_ends(result, key, least, top_value):
    longest = result.shape.index(max(result.shape))
    spots = []
    for shift in (0, 1):
        where = [jax.random.randint(jax.random.fold_in(key, axis), (), 0, length) for axis, length in enumerate(result.shape)]
        where[longest] = (where[longest] + shift) % result.shape[longest]
        spots.append(tuple(where))
    return result.at[spots[0]].set(least).at[spots[1]].set(top_value)


def block_levels(own_key, extent, cuts, smallest, largest):
    factor_of, own = 1.0, jax.random.fold_in(own_key, 6)
    for axis_at, parts in cuts:
        heights = jnp.exp(jax.random.uniform(jax.random.fold_in(own, axis_at), (parts,), jnp.float32, smallest / len(cuts), largest / len(cuts)))
        factor_of = factor_of * jnp.repeat(heights, extent[axis_at] // parts).reshape([-1 if axis == axis_at else 1 for axis in range(len(extent))])
    return factor_of


def gaussian(own_key, shape, spread, limit, cuts=(), held_as=jnp.bfloat16):
    loudness = block_levels(own_key, shape, cuts, -0.22, 0.18) if cuts else 1.0
    entries = jax.random.normal(own_key, shape, jnp.float32) * spread * loudness
    return jnp.minimum(jnp.maximum(entries, -limit), limit).astype(held_as)


def setup_inputs(seed: int = 0) -> dict:
    splits = jax.random.split(jax.random.key(seed), 18)
    return {
        "grid_state": gaussian(splits[0], (GRID, H), 1.0, 6.0, ((0, 8), (1, 4))),
        "mesh_state": gaussian(splits[1], (MESH, H), 1.0, 6.0, ((0, 8), (1, 4))),
        "enc_send": gaussian(splits[2], (H, H), H ** -0.5, 0.1875, ((1, 4),)),
        "enc_out": gaussian(splits[3], (H, H), H ** -0.5, 0.1875, ((1, 4),)),
        "proc_send": gaussian(splits[4], (H, H), H ** -0.5, 0.1875, ((1, 4),)),
        "proc_out": gaussian(splits[5], (H, H), H ** -0.5, 0.1875, ((1, 4),)),
        "dec_send": gaussian(splits[6], (H, H), H ** -0.5, 0.1875, ((1, 4),)),
        "dec_out": gaussian(splits[7], (H, H), H ** -0.5, 0.1875, ((1, 4),)),
        "g2m_index": draw_g2m_index(jax.random.fold_in(splits[17], 71), 0),
        "g2m_weight": jnp.clip(jnp.exp(math.log(4.0) - 2.7725887 * jax.random.uniform(splits[9], (K_E, MESH), jnp.float32) ** block_levels(splits[9], (K_E, MESH), ((1, 8),), -0.2, 0.2)), 0.25, 4.0),
        "g2m_count": place_ends(jax.random.randint(splits[10], (MESH,), 1, K_E + 1), jax.random.fold_in(splits[10], 1), 1, K_E).astype(jnp.int32),
        "m2m_index": draw_m2m_index(jax.random.fold_in(splits[17], 71), 0),
        "m2m_weight": jnp.clip(jnp.exp(math.log(4.0) - 2.7725887 * jax.random.uniform(splits[12], (K_M, MESH), jnp.float32) ** block_levels(splits[12], (K_M, MESH), ((1, 8),), -0.2, 0.2)), 0.25, 4.0),
        "m2m_count": place_ends(jax.random.randint(splits[13], (MESH,), 1, K_M + 1), jax.random.fold_in(splits[13], 1), 1, K_M).astype(jnp.int32),
        "m2g_index": draw_m2g_index(jax.random.fold_in(splits[17], 71), 0),
        "m2g_weight": jnp.clip(jnp.exp(math.log(4.0) - 2.7725887 * jax.random.uniform(splits[15], (K_D, GRID), jnp.float32) ** block_levels(splits[15], (K_D, GRID), ((1, 8),), -0.2, 0.2)), 0.25, 4.0),
        "m2g_count": place_ends(jax.random.randint(splits[16], (GRID,), 1, K_D + 1), jax.random.fold_in(splits[16], 1), 1, K_D).astype(jnp.int32),
    }


def messages(projected, receivers, index_block, edge_weight, counts):
    slots = index_block.shape[0]
    fetched = jnp.take(projected, index_block, axis=0).astype(jnp.float32)
    message = jax.nn.silu(fetched + receivers.astype(jnp.float32)[None]) * edge_weight[:, :, None]
    valid = jnp.arange(slots, dtype=jnp.int32)[:, None] < counts[None, :]
    summed = jnp.sum(jnp.where(valid[:, :, None], message, 0.0), axis=0)
    return (summed / counts.astype(jnp.float32)[:, None]).astype(jnp.bfloat16)


def layer(senders, receivers, w_send, w_out, index_block, edge_weight, counts):
    projected = jnp.dot(senders, w_send, preferred_element_type=jnp.float32).astype(jnp.bfloat16)
    slots = index_block.shape[0]
    per_region = receivers.shape[0] // N_REGION
    width = receivers.shape[1]
    recv_blocks = receivers.reshape(N_REGION, per_region, width)
    index_blocks = index_block.reshape(slots, N_REGION, per_region).transpose(1, 0, 2)
    weight_blocks = edge_weight.reshape(slots, N_REGION, per_region).transpose(1, 0, 2)
    count_blocks = counts.reshape(N_REGION, per_region)

    def one_block(items):
        return messages(projected, items[0], items[1], items[2], items[3])

    aggregate = lax.map(one_block, (recv_blocks, index_blocks, weight_blocks, count_blocks))
    aggregate = aggregate.reshape(receivers.shape[0], width)
    update = jnp.dot(aggregate, w_out, preferred_element_type=jnp.float32)
    return (receivers.astype(jnp.float32) + update).astype(jnp.bfloat16)


def reference(grid_state, mesh_state, enc_send, enc_out, proc_send, proc_out, dec_send, dec_out, g2m_index, g2m_weight, g2m_count, m2m_index, m2m_weight, m2m_count, m2g_index, m2g_weight, m2g_count):
    mesh_one = layer(grid_state, mesh_state, enc_send, enc_out, g2m_index, g2m_weight, g2m_count)
    mesh_next = layer(mesh_one, mesh_one, proc_send, proc_out, m2m_index, m2m_weight, m2m_count)
    grid_next = layer(mesh_next, grid_state, dec_send, dec_out, m2g_index, m2g_weight, m2g_count)
    return grid_next, mesh_next
```

```python
import functools

import jax
import jax.numpy as jnp
from jax import lax
from jax.experimental import pallas as pl
from jax.experimental.pallas import tpu as pltpu
from jax.sharding import PartitionSpec as P

SPAN = 2
WIN = 2 * SPAN + 1
OFFSETS = (1, -1, 2, -2)
CH = 4
BF = jnp.bfloat16
F32 = jnp.float32


def kernel(
    n_region,
    grid_state,
    mesh_state,
    enc_send,
    enc_out,
    proc_send,
    proc_out,
    dec_send,
    dec_out,
    ei_ref,
    ew_ref,
    ec_ref,
    pi_ref,
    pw_ref,
    pc_ref,
    di_ref,
    dw_ref,
    dc_ref,
    grid_next,
    mesh_next,
    gbuf,
    msbuf,
    eobuf,
    pobuf,
    etab,
    ptab,
    dtab,
    epos,
    ewt,
    ppos,
    pwt,
    dpos,
    dwt,
    gath,
    agg1,
    agg2,
    agg3,
    m1,
    mn,
    gs_s,
    gs_r,
    ms_s,
    ms_r,
    eo_s,
    eo_r,
    po_s,
    po_r,
    a1_s,
    a1_r,
    a2_s,
    a2_r,
    a3_s,
    a3_r,
    et_s,
    et_r,
    pt_s,
    pt_r,
    dt_s,
    dt_r,
):
    r = lax.axis_index("region")
    c = lax.axis_index("chan")
    c1 = c + 1 - 2 * (c % 2)
    c2 = (c + 2) % 4
    c3 = c2 + 1 - 2 * (c2 % 2)
    rel = (c, c1, c2, c3)
    width = grid_state.shape[1]
    g_rows = grid_state.shape[0]
    m_rows = mesh_state.shape[0]
    cr = g_rows // CH

    def inside(o):
        return jnp.logical_and(r + o >= 0, r + o < n_region)

    barrier = pltpu.get_barrier_semaphore()
    for p in (c1, c2, c3):
        pl.semaphore_signal(barrier, inc=1, device_id=(r, p), device_id_type=pl.DeviceIdType.MESH)
    count = jnp.int32(3)
    for o in OFFSETS:
        ok = inside(o)

        @pl.when(ok)
        def _(o=o):
            pl.semaphore_signal(barrier, inc=1, device_id=(r + o, c), device_id_type=pl.DeviceIdType.MESH)

        count = count + jnp.where(ok, 1, 0)
    pl.semaphore_wait(barrier, count)

    def rcopy(src, dst, ssem, rsem, dev):
        return pltpu.make_async_remote_copy(
            src_ref=src, dst_ref=dst, send_sem=ssem, recv_sem=rsem,
            device_id=dev, device_id_type=pl.DeviceIdType.MESH,
        )

    pending = []

    class Gather:
        def __init__(self, own, slot, ssem, rsem):
            self.to_core = rcopy(own, slot(0), ssem(0), rsem(0), (r, c1))
            self.to_x = rcopy(own, slot(1), ssem(1), rsem(1), (r, c2))
            self.onward = rcopy(slot(1), slot(2), ssem(2), rsem(2), (r, c1))

        def start(self):
            self.to_x.start()
            self.to_core.start()
            pending.append(self)

        def forward(self):
            self.to_x.wait_recv()
            self.onward.start()

        def finish(self):
            self.to_core.wait_recv()
            self.onward.wait_recv()

        def drain(self):
            self.to_core.wait_send()
            self.to_x.wait_send()
            self.onward.wait_send()

    def exchange(tab, ssem, rsem, d):
        return rcopy(tab(0), tab(-d), ssem(d), rsem(-d), ((r + d + n_region) % n_region, c))

    def exchange_start(tab, ssem, rsem):
        for d in OFFSETS:
            @pl.when(inside(d))
            def _(d=d):
                exchange(tab, ssem, rsem, d).start()

    def exchange_recv(tab, ssem, rsem):
        for o in OFFSETS:
            @pl.when(inside(o))
            def _(o=o):
                exchange(tab, ssem, rsem, -o).wait_recv()

    def exchange_drain(tab, ssem, rsem):
        for d in OFFSETS:
            @pl.when(inside(d))
            def _(d=d):
                exchange(tab, ssem, rsem, d).wait_send()

    grid_g = []
    for q in range(CH):
        rows = pl.ds(q * cr, cr)
        g = Gather(
            grid_state.at[rows, :],
            lambda s, q=q: gbuf.at[s, q],
            lambda s, q=q: gs_s.at[s, q],
            lambda s, q=q: gs_r.at[s, q],
        )
        g.start()
        grid_g.append(g)

    def whole(own, buf, ssem, rsem):
        return Gather(own, lambda s: buf.at[s], lambda s: ssem.at[s], lambda s: rsem.at[s])

    ms_g = whole(mesh_state, msbuf, ms_s, ms_r)
    ms_g.start()

    for o in OFFSETS:
        @pl.when(jnp.logical_not(inside(o)))
        def _(o=o):
            for q in range(CH):
                etab[q, o + SPAN] = jnp.zeros((cr, width), BF)
            ptab[o + SPAN] = jnp.zeros((m_rows, width), BF)
            dtab[o + SPAN] = jnp.zeros((m_rows, width), BF)

    def edges(idx_ref, w_ref, cnt_ref, rows_per_region, pos_ref, wt_ref):
        slots, recv = idx_ref.shape
        first = (r - SPAN) * rows_per_region
        tile = m_rows
        for t in range(recv // tile):
            cols = pl.ds(t * tile, tile)
            cnt = cnt_ref[:, cols]
            k = lax.broadcasted_iota(jnp.int32, (slots, tile), 0)
            w = jnp.where(k < cnt, w_ref[:, cols], 0.0) / cnt.astype(F32)
            p = (idx_ref[:, cols] - first).astype(F32)
            pad = jnp.zeros((128 - 2 * slots, tile), F32)
            both = jnp.concatenate([w, p, pad], axis=0).T
            for s in range(slots):
                at = pl.ds((t * slots + s) * tile, tile)
                wt_ref[at, :] = jnp.broadcast_to(both[:, s : s + 1], (tile, 128))
                pos_ref[at, :] = jnp.broadcast_to(
                    both[:, slots + s : slots + s + 1].astype(jnp.int32), (tile, 128)
                ).astype(jnp.int16)

    edges(ei_ref, ew_ref, ec_ref, g_rows, epos, ewt)
    edges(pi_ref, pw_ref, pc_ref, m_rows, ppos, pwt)
    edges(di_ref, dw_ref, dc_ref, m_rows, dpos, dwt)

    def wrows(w_ref, j):
        return w_ref[pl.ds(pl.multiple_of(rel[j] * width, width), width), :]

    def dot(a, b):
        return jnp.dot(a, b, preferred_element_type=F32)

    def pick(tab, pos_ref, lo, n, stride, base, gath_lo, first, m=512):
        table = tab[...].reshape(-1, width)
        block = tab.shape[1]

        @pl.loop(0, n // m)
        def _(i):
            p = pos_ref[pl.ds(pl.multiple_of(lo + i * m, m), m), :]
            lane = lax.broadcasted_iota(jnp.int16, (m, 128), 1)
            q = p - lane
            parts = []
            for o in range(WIN):
                for h in range(block // 128):
                    parts.append(jnp.where(q == jnp.int16(o * stride + base + h * 128), BF(1), BF(0)))
            hot = jnp.concatenate(parts, axis=1)
            got = dot(hot, table)
            at = pl.ds(pl.multiple_of(gath_lo + i * m, m), m)
            if first:
                gath[at, :] = got.astype(BF)
            else:
                gath[at, :] = (gath[at, :].astype(F32) + got).astype(BF)

    def message(recv_ref, recv_lo, wt_ref, lo, slots, out_ref, tile=32):
        @pl.loop(0, m_rows // tile)
        def _(i):
            half = recv_ref[pl.ds(pl.multiple_of(recv_lo + i * tile, tile), tile), :].astype(F32) * 0.5
            acc = jnp.zeros((tile, width), F32)
            for s in range(slots):
                g = gath[pl.ds(pl.multiple_of(s * m_rows + i * tile, tile), tile), :].astype(F32)
                h = g + half
                w = wt_ref[pl.ds(pl.multiple_of(lo + s * m_rows + i * tile, tile), tile), :]
                acc = acc + jnp.concatenate([w] * (width // 128), axis=1) * (h + h * jnp.tanh(h))
            out_ref[pl.ds(pl.multiple_of(i * tile, tile), tile), :] = acc.astype(BF)

    def etab_q(q):
        return (
            lambda o: etab.at[q, o + SPAN],
            lambda d: et_s.at[q, d + SPAN],
            lambda o: et_r.at[q, o + SPAN],
        )

    for q in range(CH):
        g = grid_g[q]
        g.forward()
        acc = dot(grid_state[pl.ds(q * cr, cr), :], wrows(enc_send, 0))
        g.to_core.wait_recv()
        acc = acc + dot(gbuf[0, q], wrows(enc_send, 1)) + dot(gbuf[1, q], wrows(enc_send, 2))
        g.onward.wait_recv()
        acc = acc + dot(gbuf[2, q], wrows(enc_send, 3))
        etab[q, SPAN] = (acc * 0.5).astype(BF)
        exchange_start(*etab_q(q))

    ms_g.forward()
    eo_g = whole(enc_out, eobuf, eo_s, eo_r)
    eo_g.start()
    po_g = whole(proc_out, pobuf, po_s, po_r)
    e_rows = epos.shape[0]
    for q in range(CH):
        exchange_recv(*etab_q(q))
        pick(etab.at[q], epos, 0, e_rows, g_rows, q * cr, 0, q == 0)
        if q == 1:
            eo_g.forward()
            po_g.start()
    message(mesh_state, 0, ewt, 0, ei_ref.shape[0], agg1.at[0])
    a_g = Gather(agg1.at[0], lambda s: agg1.at[s + 1], lambda s: a1_s.at[s], lambda s: a1_r.at[s])
    a_g.start()
    ms_g.finish()
    eo_g.finish()
    po_g.forward()
    a_g.forward()
    a_g.finish()

    def update(state, agg, w_own, w_buf, out):
        for j in range(4):
            w_ref = w_own if j == 0 else w_buf.at[j - 1]
            acc = state(j).astype(F32)
            for i in range(4):
                acc = acc + dot(agg[i], wrows(w_ref, i))
            out[j] = acc.astype(BF)

    def project(m, w_ref, tab):
        acc = dot(m[0], wrows(w_ref, 0))
        for j in range(1, 4):
            acc = acc + dot(m[j], wrows(w_ref, j))
        tab[SPAN] = (acc * 0.5).astype(BF)

    update(lambda j: mesh_state[...] if j == 0 else msbuf[j - 1], agg1, enc_out, eobuf, m1)

    project(m1, proc_send, ptab)
    pt = (lambda o: ptab.at[o + SPAN], lambda d: pt_s.at[d + SPAN], lambda o: pt_r.at[o + SPAN])
    exchange_start(*pt)
    exchange_recv(*pt)
    pick(ptab, ppos, 0, ppos.shape[0], m_rows, 0, 0, True)
    message(m1.at[0], 0, pwt, 0, pi_ref.shape[0], agg2.at[0])
    b_g = Gather(agg2.at[0], lambda s: agg2.at[s + 1], lambda s: a2_s.at[s], lambda s: a2_r.at[s])
    b_g.start()
    po_g.finish()
    b_g.forward()
    b_g.finish()
    update(lambda j: m1[j], agg2, proc_out, pobuf, mn)

    project(mn, dec_send, dtab)
    dt = (lambda o: dtab.at[o + SPAN], lambda d: dt_s.at[d + SPAN], lambda o: dt_r.at[o + SPAN])
    exchange_start(*dt)
    mesh_next[...] = mn[0]
    exchange_recv(*dt)
    tiles = g_rows // m_rows
    d_slots = di_ref.shape[0]
    per = d_slots * m_rows
    out_g = []

    def write(t):
        at = pl.ds(t * m_rows, m_rows)
        acc = grid_state[at, :].astype(F32) + dot(agg3[0, t], wrows(dec_out, 0))
        out_g[t].finish()
        for j in range(1, 4):
            acc = acc + dot(agg3[j, t], wrows(dec_out, j))
        grid_next[at, :] = acc.astype(BF)

    for t in range(tiles):
        pick(dtab, dpos, t * per, per, m_rows, 0, 0, True)
        message(grid_state, t * m_rows, dwt, t * per, d_slots, agg3.at[0, t])
        g = Gather(
            agg3.at[0, t],
            lambda s, t=t: agg3.at[s + 1, t],
            lambda s, t=t: a3_s.at[s, t],
            lambda s, t=t: a3_r.at[s, t],
        )
        g.start()
        out_g.append(g)
        if t > 0:
            out_g[t - 1].forward()
    for t in range(tiles):
        if t == tiles - 1:
            out_g[t].forward()
        write(t)

    for g in pending:
        g.drain()
    for q in range(CH):
        exchange_drain(*etab_q(q))
    exchange_drain(*pt)
    exchange_drain(*dt)


def shards(*args):
    grid_state, mesh_state = args[:2]
    n_region = lax.axis_size("region")
    assert lax.axis_size("chan") == 4
    g_rows, width = grid_state.shape
    m_rows = mesh_state.shape[0]
    full = args[2].shape[0]
    cr = g_rows // CH
    tiles = g_rows // m_rows
    ke, kp, kd = args[8].shape[0], args[11].shape[0], args[14].shape[0]
    args = list(args)
    for i in (10, 13, 16):
        args[i] = args[i].reshape(1, -1)
    dma = pltpu.SemaphoreType.DMA
    V = pltpu.VMEM
    lanes = 128
    scratch = [
        V((3, CH, cr, width), BF),
        V((3, m_rows, width), BF),
        V((3, full, width), BF),
        V((3, full, width), BF),
        V((CH, WIN, cr, width), BF),
        V((WIN, m_rows, width), BF),
        V((WIN, m_rows, width), BF),
        V((ke * m_rows, lanes), jnp.int16),
        V((ke * m_rows, lanes), F32),
        V((kp * m_rows, lanes), jnp.int16),
        V((kp * m_rows, lanes), F32),
        V((kd * g_rows, lanes), jnp.int16),
        V((kd * g_rows, lanes), F32),
        V((ke * m_rows, width), BF),
        V((4, m_rows, width), BF),
        V((4, m_rows, width), BF),
        V((4, tiles, m_rows, width), BF),
        V((4, m_rows, width), BF),
        V((4, m_rows, width), BF),
        dma((3, CH)),
        dma((3, CH)),
        dma((3,)),
        dma((3,)),
        dma((3,)),
        dma((3,)),
        dma((3,)),
        dma((3,)),
        dma((3,)),
        dma((3,)),
        dma((3,)),
        dma((3,)),
        dma((3, tiles)),
        dma((3, tiles)),
        dma((CH, WIN)),
        dma((CH, WIN)),
        dma((WIN,)),
        dma((WIN,)),
        dma((WIN,)),
        dma((WIN,)),
    ]
    return pl.pallas_call(
        functools.partial(kernel, n_region),
        out_shape=(
            jax.ShapeDtypeStruct((g_rows, width), BF),
            jax.ShapeDtypeStruct((m_rows, width), BF),
        ),
        in_specs=[pl.BlockSpec(memory_space=pltpu.VMEM)] * 17,
        out_specs=(pl.BlockSpec(memory_space=pltpu.VMEM),) * 2,
        scratch_shapes=scratch,
        compiler_params=pltpu.CompilerParams(
            collective_id=0, has_side_effects=True, vmem_limit_bytes=56 * 1024 * 1024
        ),
    )(*args)


def solution(mesh):
    placed = (
        P("region", "chan"),
        P("region", "chan"),
        P(None, "chan"),
        P(None, "chan"),
        P(None, "chan"),
        P(None, "chan"),
        P(None, "chan"),
        P(None, "chan"),
        P(None, "region"),
        P(None, "region"),
        P("region"),
        P(None, "region"),
        P(None, "region"),
        P("region"),
        P(None, "region"),
        P(None, "region"),
        P("region"),
    )
    return jax.shard_map(
        shards,
        mesh=mesh,
        in_specs=placed,
        out_specs=(P("region", "chan"), P("region", "chan")),
        check_vma=False,
    )
```

```python
import functools

import jax
import jax.numpy as jnp
from jax import lax
from jax.experimental import pallas as pl
from jax.experimental.pallas import tpu as pltpu
from jax.sharding import PartitionSpec as P

SPAN = 2
WIN = 2 * SPAN + 1
OFFSETS = (1, -1, 2, -2)
CH = 4
BF = jnp.bfloat16
F32 = jnp.float32


def kernel(
    n_region,
    grid_state,
    mesh_state,
    enc_send,
    enc_out,
    proc_send,
    proc_out,
    dec_send,
    dec_out,
    ei_ref,
    ew_ref,
    ec_ref,
    pi_ref,
    pw_ref,
    pc_ref,
    di_ref,
    dw_ref,
    dc_ref,
    grid_next,
    mesh_next,
    gbuf,
    msbuf,
    eobuf,
    pobuf,
    wms,
    wi,
    ww,
    wc,
    part,
    precv,
    own32,
    etab,
    ptab,
    dtab,
    epos,
    ewt,
    ppos,
    pwt,
    dpos,
    dwt,
    gath,
    got,
    agg1,
    agg2,
    agg3,
    m1,
    mn,
    gs_s,
    gs_r,
    ms_s,
    ms_r,
    eo_s,
    eo_r,
    po_s,
    po_r,
    a1_s,
    a1_r,
    a2_s,
    a2_r,
    a3_s,
    a3_r,
    wn_s,
    wn_r,
    pp_s,
    pp_r,
    pt_s,
    pt_r,
    dt_s,
    dt_r,
):
    r = lax.axis_index("region")
    c = lax.axis_index("chan")
    c1 = c + 1 - 2 * (c % 2)
    c2 = (c + 2) % 4
    c3 = c2 + 1 - 2 * (c2 % 2)
    rel = (c, c1, c2, c3)
    width = grid_state.shape[1]
    g_rows = grid_state.shape[0]
    m_rows = mesh_state.shape[0]
    cr = g_rows // CH

    def inside(o):
        return jnp.logical_and(r + o >= 0, r + o < n_region)

    barrier = pltpu.get_barrier_semaphore()
    for p in (c1, c2, c3):
        pl.semaphore_signal(barrier, inc=1, device_id=(r, p), device_id_type=pl.DeviceIdType.MESH)
    count = jnp.int32(3)
    for o in OFFSETS:
        ok = inside(o)

        @pl.when(ok)
        def _(o=o):
            pl.semaphore_signal(barrier, inc=1, device_id=(r + o, c), device_id_type=pl.DeviceIdType.MESH)

        count = count + jnp.where(ok, 1, 0)
    pl.semaphore_wait(barrier, count)

    def rcopy(src, dst, ssem, rsem, dev):
        return pltpu.make_async_remote_copy(
            src_ref=src, dst_ref=dst, send_sem=ssem, recv_sem=rsem,
            device_id=dev, device_id_type=pl.DeviceIdType.MESH,
        )

    pending = []

    class Gather:
        def __init__(self, own, slot, ssem, rsem):
            self.to_core = rcopy(own, slot(0), ssem(0), rsem(0), (r, c1))
            self.to_x = rcopy(own, slot(1), ssem(1), rsem(1), (r, c2))
            self.onward = rcopy(slot(1), slot(2), ssem(2), rsem(2), (r, c1))

        def start(self):
            self.to_x.start()
            self.to_core.start()
            pending.append(self)

        def forward(self):
            self.to_x.wait_recv()
            self.onward.start()

        def finish(self):
            self.to_core.wait_recv()
            self.onward.wait_recv()

        def drain(self):
            self.to_core.wait_send()
            self.to_x.wait_send()
            self.onward.wait_send()

    def exchange(tab, ssem, rsem, d):
        return rcopy(tab(0), tab(-d), ssem(d), rsem(-d), ((r + d + n_region) % n_region, c))

    def exchange_start(tab, ssem, rsem):
        for d in OFFSETS:
            @pl.when(inside(d))
            def _(d=d):
                exchange(tab, ssem, rsem, d).start()

    def exchange_recv(tab, ssem, rsem):
        for o in OFFSETS:
            @pl.when(inside(o))
            def _(o=o):
                exchange(tab, ssem, rsem, -o).wait_recv()

    def exchange_drain(tab, ssem, rsem):
        for d in OFFSETS:
            @pl.when(inside(d))
            def _(d=d):
                exchange(tab, ssem, rsem, d).wait_send()

    window = []
    for at, (own, buf) in enumerate(((ei_ref, wi), (ew_ref, ww), (ec_ref, wc), (mesh_state, wms))):
        window.append((
            lambda o, own=own, buf=buf: own if o == 0 else buf.at[o + SPAN],
            lambda d, at=at: wn_s.at[at, d + SPAN],
            lambda o, at=at: wn_r.at[at, o + SPAN],
        ))
    for w in window[:3]:
        exchange_start(*w)

    grid_g = []
    for q in range(CH):
        rows = pl.ds(q * cr, cr)
        g = Gather(
            grid_state.at[rows, :],
            lambda s, q=q: gbuf.at[s, q],
            lambda s, q=q: gs_s.at[s, q],
            lambda s, q=q: gs_r.at[s, q],
        )
        g.start()
        grid_g.append(g)

    def whole(own, buf, ssem, rsem):
        return Gather(own, lambda s: buf.at[s], lambda s: ssem.at[s], lambda s: rsem.at[s])

    ms_g = whole(mesh_state, msbuf, ms_s, ms_r)
    ms_g.start()
    exchange_start(*window[3])

    for o in OFFSETS:
        @pl.when(jnp.logical_not(inside(o)))
        def _(o=o):
            precv[o + SPAN] = jnp.zeros((m_rows, width), BF)
            ptab[o + SPAN] = jnp.zeros((m_rows, width), BF)
            dtab[o + SPAN] = jnp.zeros((m_rows, width), BF)

    def edges(idx, w_all, cnt_all, first, length, tile, pos_ref, wt_ref):
        slots, recv = idx.shape
        for t in range(recv // m_rows):
            cols = slice(t * m_rows, (t + 1) * m_rows)
            cnt = cnt_all[:, cols]
            p = idx[:, cols] - first
            k = lax.broadcasted_iota(jnp.int32, (slots, m_rows), 0)
            live = (k < cnt) & (p >= 0) & (p < length)
            w = jnp.where(live, w_all[:, cols], 0.0) / cnt.astype(F32)
            pad = jnp.zeros((128 - 2 * slots, m_rows), F32)
            both = jnp.concatenate([w, p.astype(F32), pad], axis=0).T
            for u in range(m_rows // tile):
                mine = both[u * tile : (u + 1) * tile, :]
                for s in range(slots):
                    at = pl.ds(((t * (m_rows // tile) + u) * slots + s) * tile, tile)
                    wt_ref[at, :] = jnp.broadcast_to(mine[:, s : s + 1], (tile, 128))
                    pos_ref[at, :] = jnp.broadcast_to(
                        mine[:, slots + s : slots + s + 1].astype(jnp.int32), (tile, 128)
                    ).astype(jnp.int16)

    def wrows(w_ref, j):
        return w_ref[pl.ds(pl.multiple_of(rel[j] * width, width), width), :]

    def dot(a, b):
        return jnp.dot(a, b, preferred_element_type=F32)

    def hot(pos_ref, at, m, base, length):
        q = pos_ref[at, :] - lax.broadcasted_iota(jnp.int16, (m, 128), 1)
        parts = [
            jnp.where(q == jnp.int16(base + lane), BF(1), BF(0)) for lane in range(0, length, 128)
        ]
        return jnp.concatenate(parts, axis=1)

    def messages(table, base, pos_ref, wt_ref, lo, slots, tile, tiles, recv_ref, recv_lo, out_ref, prior=None, sub=32):
        m = slots * tile

        @pl.loop(0, tiles)
        def _(i):
            at = pl.ds(pl.multiple_of(lo + i * m, m), m)
            new = dot(hot(pos_ref, at, m, base, table.shape[0]), table)
            if prior is not None:
                new = new + prior[pl.ds(pl.multiple_of(i * m, m), m), :].astype(F32)
            got[...] = new

            @pl.loop(0, tile // sub)
            def _(j):
                off = pl.multiple_of(j * sub, sub)
                rows = pl.ds(pl.multiple_of(recv_lo + i * tile + off, sub), sub)
                half = recv_ref[rows, :].astype(F32) * 0.5
                acc = jnp.zeros((sub, width), F32)
                for s in range(slots):
                    h = got[pl.ds(pl.multiple_of(s * tile + off, sub), sub), :] + half
                    w = wt_ref[pl.ds(pl.multiple_of(lo + i * m + s * tile + off, sub), sub), :]
                    acc = acc + jnp.concatenate([w] * (width // 128), axis=1) * (h + h * jnp.tanh(h))
                out_ref[pl.ds(pl.multiple_of(i * tile + off, sub), sub), :] = acc.astype(out_ref.dtype)

    ke, kp, kd = ei_ref.shape[0], pi_ref.shape[0], di_ref.shape[0]
    e_tile, p_tile, d_tile = got.shape[0] // ke, got.shape[0] // kp, got.shape[0] // kd
    e_rows = ke * m_rows
    order = (2, -2, 1, -1, 0)

    def here(o, body):
        if o == 0:
            body()
        else:
            pl.when(inside(o))(body)

    def window_edges(o):
        def body():
            if o == 0:
                data = ei_ref[...], ew_ref[...], ec_ref[...]
            else:
                for w in window[:3]:
                    exchange(*w, -o).wait_recv()
                data = wi[o + SPAN], ww[o + SPAN], wc[o + SPAN]
            edges(*data, r * g_rows, g_rows, e_tile, epos.at[o + SPAN], ewt.at[o + SPAN])

        here(o, body)

    def project_grid(q):
        g = grid_g[q]
        acc = dot(grid_state[pl.ds(q * cr, cr), :], wrows(enc_send, 0))
        g.to_core.wait_recv()
        acc = acc + dot(gbuf[0, q], wrows(enc_send, 1)) + dot(gbuf[1, q], wrows(enc_send, 2))
        g.onward.wait_recv()
        acc = acc + dot(gbuf[2, q], wrows(enc_send, 3))
        etab[pl.ds(q * cr, cr), :] = (acc * 0.5).astype(BF)

    early = g_rows // 2

    def first_half(o):
        def body():
            m = 2048

            @pl.loop(0, e_rows // m)
            def _(i):
                at = pl.ds(pl.multiple_of(i * m, m), m)
                gath[o + SPAN, at, :] = dot(
                    hot(epos.at[o + SPAN], at, m, 0, early), etab[pl.ds(0, early), :]
                ).astype(BF)

        here(o, body)

    def back(d):
        return rcopy(part.at[d + SPAN], precv.at[SPAN - d], pp_s.at[d + SPAN], pp_r.at[SPAN - d],
                     ((r + d + n_region) % n_region, c))

    def second_half(o):
        def body():
            if o != 0:
                exchange(*window[3], -o).wait_recv()
            messages(
                etab[pl.ds(early, g_rows - early), :], early, epos.at[o + SPAN], ewt.at[o + SPAN], 0,
                ke, e_tile, m_rows // e_tile, mesh_state if o == 0 else wms.at[o + SPAN], 0,
                own32 if o == 0 else part.at[o + SPAN], gath.at[o + SPAN],
            )
            if o != 0:
                back(o).start()

        here(o, body)

    window_edges(0)
    grid_g[0].forward()
    window_edges(1)
    project_grid(0)
    grid_g[1].forward()
    window_edges(-1)
    project_grid(1)
    grid_g[2].forward()
    window_edges(2)
    window_edges(-2)
    for o in order:
        first_half(o)
        if o == -2:
            grid_g[3].forward()
            ms_g.forward()
    eo_g = whole(enc_out, eobuf, eo_s, eo_r)
    eo_g.start()
    project_grid(2)
    project_grid(3)
    for o in order:
        second_half(o)
        if o == 1:
            eo_g.forward()
    po_g = whole(proc_out, pobuf, po_s, po_r)
    total = own32[...]
    for o in OFFSETS:
        @pl.when(inside(o))
        def _(o=o):
            back(-o).wait_recv()
    for o in OFFSETS:
        total = total + precv[o + SPAN].astype(F32)
    agg1[0] = total.astype(BF)
    a_g = Gather(agg1.at[0], lambda s: agg1.at[s + 1], lambda s: a1_s.at[s], lambda s: a1_r.at[s])
    a_g.start()
    edges(pi_ref[...], pw_ref[...], pc_ref[...], (r - SPAN) * m_rows, WIN * m_rows, p_tile, ppos, pwt)
    ms_g.finish()
    eo_g.finish()
    a_g.forward()
    a_g.finish()
    po_g.start()

    def update(state, agg, w_own, w_buf, out):
        for j in range(4):
            w_ref = w_own if j == 0 else w_buf.at[j - 1]
            acc = state(j).astype(F32)
            for i in range(4):
                acc = acc + dot(agg[i], wrows(w_ref, i))
            out[j] = acc.astype(BF)

    def project(m, w_ref, tab):
        acc = dot(m[0], wrows(w_ref, 0))
        for j in range(1, 4):
            acc = acc + dot(m[j], wrows(w_ref, j))
        tab[SPAN] = (acc * 0.5).astype(BF)

    update(lambda j: mesh_state[...] if j == 0 else msbuf[j - 1], agg1, enc_out, eobuf, m1)

    project(m1, proc_send, ptab)
    pt = (lambda o: ptab.at[o + SPAN], lambda d: pt_s.at[d + SPAN], lambda o: pt_r.at[o + SPAN])
    exchange_start(*pt)
    edges(di_ref[...], dw_ref[...], dc_ref[...], (r - SPAN) * m_rows, WIN * m_rows, d_tile, dpos, dwt)
    exchange_recv(*pt)
    messages(
        ptab[...].reshape(-1, width), 0, ppos, pwt, 0, kp, p_tile, m_rows // p_tile, m1.at[0], 0, agg2.at[0]
    )
    po_g.forward()
    b_g = Gather(agg2.at[0], lambda s: agg2.at[s + 1], lambda s: a2_s.at[s], lambda s: a2_r.at[s])
    b_g.start()
    po_g.finish()
    b_g.forward()
    b_g.finish()
    update(lambda j: m1[j], agg2, proc_out, pobuf, mn)

    project(mn, dec_send, dtab)
    dt = (lambda o: dtab.at[o + SPAN], lambda d: dt_s.at[d + SPAN], lambda o: dt_r.at[o + SPAN])
    exchange_start(*dt)
    mesh_next[...] = mn[0]
    exchange_recv(*dt)
    tiles = g_rows // m_rows
    per = kd * m_rows
    out_g = []

    def write(t):
        at = pl.ds(t * m_rows, m_rows)
        acc = grid_state[at, :].astype(F32) + dot(agg3[0, t], wrows(dec_out, 0))
        out_g[t].finish()
        for j in range(1, 4):
            acc = acc + dot(agg3[j, t], wrows(dec_out, j))
        grid_next[at, :] = acc.astype(BF)

    for t in range(tiles):
        messages(
            dtab[...].reshape(-1, width), 0, dpos, dwt, t * per, kd, d_tile, m_rows // d_tile,
            grid_state, t * m_rows, agg3.at[0, t],
        )
        g = Gather(
            agg3.at[0, t],
            lambda s, t=t: agg3.at[s + 1, t],
            lambda s, t=t: a3_s.at[s, t],
            lambda s, t=t: a3_r.at[s, t],
        )
        g.start()
        out_g.append(g)
        if t > 0:
            out_g[t - 1].forward()
    for t in range(tiles):
        if t == tiles - 1:
            out_g[t].forward()
        write(t)

    for g in pending:
        g.drain()
    for w in window:
        exchange_drain(*w)
    for d in OFFSETS:
        @pl.when(inside(d))
        def _(d=d):
            back(d).wait_send()
    exchange_drain(*pt)
    exchange_drain(*dt)


def shards(*args):
    grid_state, mesh_state = args[:2]
    n_region = lax.axis_size("region")
    assert lax.axis_size("chan") == 4
    g_rows, width = grid_state.shape
    m_rows = mesh_state.shape[0]
    full = args[2].shape[0]
    cr = g_rows // CH
    tiles = g_rows // m_rows
    ke, kp, kd = args[8].shape[0], args[11].shape[0], args[14].shape[0]
    args = list(args)
    for i in (10, 13, 16):
        args[i] = args[i].reshape(1, -1)
    dma = pltpu.SemaphoreType.DMA
    V = pltpu.VMEM
    lanes = 128
    scratch = [
        V((3, CH, cr, width), BF),
        V((3, m_rows, width), BF),
        V((3, full, width), BF),
        V((3, full, width), BF),
        V((WIN, m_rows, width), BF),
        V((WIN, ke, m_rows), jnp.int32),
        V((WIN, ke, m_rows), F32),
        V((WIN, 1, m_rows), jnp.int32),
        V((WIN, m_rows, width), BF),
        V((WIN, m_rows, width), BF),
        V((m_rows, width), F32),
        V((g_rows, width), BF),
        V((WIN, m_rows, width), BF),
        V((WIN, m_rows, width), BF),
        V((WIN, ke * m_rows, lanes), jnp.int16),
        V((WIN, ke * m_rows, lanes), F32),
        V((kp * m_rows, lanes), jnp.int16),
        V((kp * m_rows, lanes), F32),
        V((kd * g_rows, lanes), jnp.int16),
        V((kd * g_rows, lanes), F32),
        V((WIN, ke * m_rows, width), BF),
        V((1024, width), F32),
        V((4, m_rows, width), BF),
        V((4, m_rows, width), BF),
        V((4, tiles, m_rows, width), BF),
        V((4, m_rows, width), BF),
        V((4, m_rows, width), BF),
        dma((3, CH)),
        dma((3, CH)),
        dma((3,)),
        dma((3,)),
        dma((3,)),
        dma((3,)),
        dma((3,)),
        dma((3,)),
        dma((3,)),
        dma((3,)),
        dma((3,)),
        dma((3,)),
        dma((3, tiles)),
        dma((3, tiles)),
        dma((4, WIN)),
        dma((4, WIN)),
        dma((WIN,)),
        dma((WIN,)),
        dma((WIN,)),
        dma((WIN,)),
        dma((WIN,)),
        dma((WIN,)),
    ]
    return pl.pallas_call(
        functools.partial(kernel, n_region),
        out_shape=(
            jax.ShapeDtypeStruct((g_rows, width), BF),
            jax.ShapeDtypeStruct((m_rows, width), BF),
        ),
        in_specs=[pl.BlockSpec(memory_space=pltpu.VMEM)] * 17,
        out_specs=(pl.BlockSpec(memory_space=pltpu.VMEM),) * 2,
        scratch_shapes=scratch,
        compiler_params=pltpu.CompilerParams(
            collective_id=0, has_side_effects=True, vmem_limit_bytes=56 * 1024 * 1024
        ),
    )(*args)


def solution(mesh):
    placed = (
        P("region", "chan"),
        P("region", "chan"),
        P(None, "chan"),
        P(None, "chan"),
        P(None, "chan"),
        P(None, "chan"),
        P(None, "chan"),
        P(None, "chan"),
        P(None, "region"),
        P(None, "region"),
        P("region"),
        P(None, "region"),
        P(None, "region"),
        P("region"),
        P(None, "region"),
        P(None, "region"),
        P("region"),
    )
    return jax.shard_map(
        shards,
        mesh=mesh,
        in_specs=placed,
        out_specs=(P("region", "chan"), P("region", "chan")),
        check_vma=False,
    )
```

```python
import functools

import jax
import jax.numpy as jnp
from jax import lax
from jax.experimental import pallas as pl
from jax.experimental.pallas import tpu as pltpu
from jax.sharding import PartitionSpec as P

SPAN = 2
WIN = 2 * SPAN + 1
OFFSETS = (1, -1, 2, -2)
CH = 4
BF = jnp.bfloat16
F32 = jnp.float32


def kernel(
    n_region,
    grid_state,
    mesh_state,
    enc_send,
    enc_out_hbm,
    proc_send_hbm,
    proc_out_hbm,
    dec_send_hbm,
    dec_out_hbm,
    ei_ref,
    ew_ref,
    ec_ref,
    pi_ref,
    pw_ref,
    pc_ref,
    di_ref,
    dw_ref,
    dc_ref,
    grid_next,
    mesh_next,
    enc_out,
    proc_send,
    proc_out,
    dec_send,
    dec_out,
    load_sem,
    gbuf,
    msbuf,
    eobuf,
    pobuf,
    wms,
    wi,
    ww,
    wc,
    part,
    precv,
    own32,
    etab,
    ptab,
    dtab,
    epos,
    ewt,
    ppos,
    pwt,
    dpos,
    dwt,
    gath,
    got,
    agg1,
    agg2,
    agg3,
    m1,
    mn,
    gs_s,
    gs_r,
    ms_s,
    ms_r,
    eo_s,
    eo_r,
    po_s,
    po_r,
    a1_s,
    a1_r,
    a2_s,
    a2_r,
    a3_s,
    a3_r,
    wn_s,
    wn_r,
    pp_s,
    pp_r,
    pt_s,
    pt_r,
    dt_s,
    dt_r,
):
    r = lax.axis_index("region")
    c = lax.axis_index("chan")
    c1 = c + 1 - 2 * (c % 2)
    c2 = (c + 2) % 4
    c3 = c2 + 1 - 2 * (c2 % 2)
    rel = (c, c1, c2, c3)
    width = grid_state.shape[1]
    g_rows = grid_state.shape[0]
    m_rows = mesh_state.shape[0]
    cr = g_rows // CH

    def inside(o):
        return jnp.logical_and(r + o >= 0, r + o < n_region)

    barrier = pltpu.get_barrier_semaphore()
    for p in (c1, c2, c3):
        pl.semaphore_signal(barrier, inc=1, device_id=(r, p), device_id_type=pl.DeviceIdType.MESH)
    count = jnp.int32(3)
    for o in OFFSETS:
        ok = inside(o)

        @pl.when(ok)
        def _(o=o):
            pl.semaphore_signal(barrier, inc=1, device_id=(r + o, c), device_id_type=pl.DeviceIdType.MESH)

        count = count + jnp.where(ok, 1, 0)
    pl.semaphore_wait(barrier, count)

    def rcopy(src, dst, ssem, rsem, dev):
        return pltpu.make_async_remote_copy(
            src_ref=src, dst_ref=dst, send_sem=ssem, recv_sem=rsem,
            device_id=dev, device_id_type=pl.DeviceIdType.MESH,
        )

    pending = []

    class Gather:
        def __init__(self, own, slot, ssem, rsem):
            self.to_core = rcopy(own, slot(0), ssem(0), rsem(0), (r, c1))
            self.to_x = rcopy(own, slot(1), ssem(1), rsem(1), (r, c2))
            self.onward = rcopy(slot(1), slot(2), ssem(2), rsem(2), (r, c1))

        def start(self):
            self.to_x.start()
            self.to_core.start()
            pending.append(self)

        def forward(self):
            self.to_x.wait_recv()
            self.onward.start()

        def finish(self):
            self.to_core.wait_recv()
            self.onward.wait_recv()

        def drain(self):
            self.to_core.wait_send()
            self.to_x.wait_send()
            self.onward.wait_send()

    def exchange(tab, ssem, rsem, d):
        return rcopy(tab(0), tab(-d), ssem(d), rsem(-d), ((r + d + n_region) % n_region, c))

    def exchange_start(tab, ssem, rsem):
        for d in OFFSETS:
            @pl.when(inside(d))
            def _(d=d):
                exchange(tab, ssem, rsem, d).start()

    def exchange_recv(tab, ssem, rsem):
        for o in OFFSETS:
            @pl.when(inside(o))
            def _(o=o):
                exchange(tab, ssem, rsem, -o).wait_recv()

    def exchange_drain(tab, ssem, rsem):
        for d in OFFSETS:
            @pl.when(inside(d))
            def _(d=d):
                exchange(tab, ssem, rsem, d).wait_send()

    window = []
    for at, (own, buf) in enumerate(((ei_ref, wi), (ew_ref, ww), (ec_ref, wc), (mesh_state, wms))):
        window.append((
            lambda o, own=own, buf=buf: own if o == 0 else buf.at[o + SPAN],
            lambda d, at=at: wn_s.at[at, d + SPAN],
            lambda o, at=at: wn_r.at[at, o + SPAN],
        ))
    for w in window[:3]:
        exchange_start(*w)

    loads = [
        pltpu.make_async_copy(a, b, load_sem.at[i])
        for i, (a, b) in enumerate((
            (enc_out_hbm, enc_out), (proc_out_hbm, proc_out), (proc_send_hbm, proc_send),
            (dec_send_hbm, dec_send), (dec_out_hbm, dec_out),
        ))
    ]

    grid_g = []
    for q in range(CH):
        rows = pl.ds(q * cr, cr)
        g = Gather(
            grid_state.at[rows, :],
            lambda s, q=q: gbuf.at[s, q],
            lambda s, q=q: gs_s.at[s, q],
            lambda s, q=q: gs_r.at[s, q],
        )
        g.start()
        grid_g.append(g)

    def whole(own, buf, ssem, rsem):
        return Gather(own, lambda s: buf.at[s], lambda s: ssem.at[s], lambda s: rsem.at[s])

    ms_g = whole(mesh_state, msbuf, ms_s, ms_r)
    ms_g.start()
    exchange_start(*window[3])
    for load in loads:
        load.start()

    for o in OFFSETS:
        @pl.when(jnp.logical_not(inside(o)))
        def _(o=o):
            precv[o + SPAN] = jnp.zeros((m_rows, width), BF)
            ptab[o + SPAN] = jnp.zeros((m_rows, width), BF)
            dtab[o + SPAN] = jnp.zeros((m_rows, width), BF)

    def edges(idx, w_all, cnt_all, first, length, tile, pos_ref, wt_ref):
        slots, recv = idx.shape
        for t in range(recv // m_rows):
            cols = slice(t * m_rows, (t + 1) * m_rows)
            cnt = cnt_all[:, cols]
            p = idx[:, cols] - first
            k = lax.broadcasted_iota(jnp.int32, (slots, m_rows), 0)
            live = (k < cnt) & (p >= 0) & (p < length)
            w = jnp.where(live, w_all[:, cols], 0.0) / cnt.astype(F32)
            pad = jnp.zeros((128 - 2 * slots, m_rows), F32)
            both = jnp.concatenate([w, p.astype(F32), pad], axis=0).T
            for u in range(m_rows // tile):
                mine = both[u * tile : (u + 1) * tile, :]
                for s in range(slots):
                    at = pl.ds(((t * (m_rows // tile) + u) * slots + s) * tile, tile)
                    wt_ref[at, :] = jnp.broadcast_to(mine[:, s : s + 1], (tile, 128)).astype(BF)
                    pos_ref[at, :] = jnp.broadcast_to(
                        mine[:, slots + s : slots + s + 1].astype(jnp.int32), (tile, 128)
                    ).astype(jnp.int16)

    def wrows(w_ref, j):
        return w_ref[pl.ds(pl.multiple_of(rel[j] * width, width), width), :]

    def dot(a, b):
        return jnp.dot(a, b, preferred_element_type=F32)

    def hot(pos_ref, at, m, base, length):
        q = pos_ref[at, :] - lax.broadcasted_iota(jnp.int16, (m, 128), 1)
        parts = [
            jnp.where(q == jnp.int16(base + lane), BF(1), BF(0)) for lane in range(0, length, 128)
        ]
        return jnp.concatenate(parts, axis=1)

    def messages(table, base, pos_ref, wt_ref, lo, slots, tile, tiles, recv_ref, recv_lo, out_ref, prior=None, sub=32):
        m = slots * tile

        @pl.loop(0, tiles)
        def _(i):
            at = pl.ds(pl.multiple_of(lo + i * m, m), m)
            got[pl.ds(0, m), :] = dot(hot(pos_ref, at, m, base, table.shape[0]), table).astype(BF)
            for off in range(0, tile, sub):
                rows = pl.ds(pl.multiple_of(recv_lo + i * tile + off, sub), sub)
                half = recv_ref[rows, :] * BF(0.5)
                acc = jnp.zeros((sub, width), F32)
                for s in range(0, slots, 4):
                    four = []
                    for z in range(s, s + 4):
                        h = got[pl.ds(z * tile + off, sub), :]
                        if prior is not None:
                            h = h + prior[pl.ds(pl.multiple_of(i * m + z * tile + off, sub), sub), :]
                        h = h + half
                        w = wt_ref[pl.ds(pl.multiple_of(lo + i * m + z * tile + off, sub), sub), :]
                        w = jnp.concatenate([w] * (width // 128), axis=1)
                        four.append(w * (h + h * jnp.tanh(h)))
                    acc = acc + ((four[0] + four[1]) + (four[2] + four[3])).astype(F32)
                out_ref[pl.ds(pl.multiple_of(i * tile + off, sub), sub), :] = acc.astype(out_ref.dtype)

    ke, kp, kd = ei_ref.shape[0], pi_ref.shape[0], di_ref.shape[0]
    e_tile, p_tile, d_tile = 2048 // ke, 1024 // kp, 1024 // kd
    e_rows = ke * m_rows
    order = (2, -2, 1, -1, 0)

    def here(o, body):
        if o == 0:
            body()
        else:
            pl.when(inside(o))(body)

    def window_edges(o):
        def body():
            if o == 0:
                data = ei_ref[...], ew_ref[...], ec_ref[...]
            else:
                for w in window[:3]:
                    exchange(*w, -o).wait_recv()
                data = wi[o + SPAN], ww[o + SPAN], wc[o + SPAN]
            edges(*data, r * g_rows, g_rows, e_tile, epos.at[o + SPAN], ewt.at[o + SPAN])

        here(o, body)

    def project_grid(q):
        g = grid_g[q]
        acc = dot(grid_state[pl.ds(q * cr, cr), :], wrows(enc_send, 0))
        g.to_core.wait_recv()
        acc = acc + dot(gbuf[0, q], wrows(enc_send, 1)) + dot(gbuf[1, q], wrows(enc_send, 2))
        g.onward.wait_recv()
        acc = acc + dot(gbuf[2, q], wrows(enc_send, 3))
        etab[pl.ds(q * cr, cr), :] = (acc * 0.5).astype(BF)

    early = g_rows // 2

    def first_half(o):
        def body():
            m = 2048

            @pl.loop(0, e_rows // m)
            def _(i):
                at = pl.ds(pl.multiple_of(i * m, m), m)
                gath[o + SPAN, at, :] = dot(
                    hot(epos.at[o + SPAN], at, m, 0, early), etab[pl.ds(0, early), :]
                ).astype(BF)

        here(o, body)

    def back(d):
        return rcopy(part.at[d + SPAN], precv.at[SPAN - d], pp_s.at[d + SPAN], pp_r.at[SPAN - d],
                     ((r + d + n_region) % n_region, c))

    def second_half(o):
        def body():
            if o != 0:
                exchange(*window[3], -o).wait_recv()
            messages(
                etab[pl.ds(early, g_rows - early), :], early, epos.at[o + SPAN], ewt.at[o + SPAN], 0,
                ke, e_tile, m_rows // e_tile, mesh_state if o == 0 else wms.at[o + SPAN], 0,
                own32 if o == 0 else part.at[o + SPAN], gath.at[o + SPAN],
            )
            if o != 0:
                back(o).start()

        here(o, body)

    window_edges(0)
    grid_g[0].forward()
    window_edges(1)
    project_grid(0)
    grid_g[1].forward()
    window_edges(-1)
    project_grid(1)
    grid_g[2].forward()
    window_edges(2)
    window_edges(-2)
    for o in order:
        first_half(o)
        if o == -2:
            grid_g[3].forward()
            ms_g.forward()
    for load in loads:
        load.wait()
    eo_g = whole(enc_out, eobuf, eo_s, eo_r)
    eo_g.start()
    project_grid(2)
    project_grid(3)
    for o in order:
        second_half(o)
        if o == 1:
            eo_g.forward()
    po_g = whole(proc_out, pobuf, po_s, po_r)
    total = own32[...]
    for o in OFFSETS:
        @pl.when(inside(o))
        def _(o=o):
            back(-o).wait_recv()
    for o in OFFSETS:
        total = total + precv[o + SPAN].astype(F32)
    agg1[0] = total.astype(BF)
    a_g = Gather(agg1.at[0], lambda s: agg1.at[s + 1], lambda s: a1_s.at[s], lambda s: a1_r.at[s])
    a_g.start()
    edges(pi_ref[...], pw_ref[...], pc_ref[...], (r - SPAN) * m_rows, WIN * m_rows, p_tile, ppos, pwt)
    ms_g.finish()
    eo_g.finish()
    a_g.forward()
    a_g.finish()
    po_g.start()

    def update(state, agg, w_own, w_buf, out):
        for j in range(4):
            w_ref = w_own if j == 0 else w_buf.at[j - 1]
            acc = state(j).astype(F32)
            for i in range(4):
                acc = acc + dot(agg[i], wrows(w_ref, i))
            out[j] = acc.astype(BF)

    def project(m, w_ref, tab):
        acc = dot(m[0], wrows(w_ref, 0))
        for j in range(1, 4):
            acc = acc + dot(m[j], wrows(w_ref, j))
        tab[SPAN] = (acc * 0.5).astype(BF)

    update(lambda j: mesh_state[...] if j == 0 else msbuf[j - 1], agg1, enc_out, eobuf, m1)

    project(m1, proc_send, ptab)
    pt = (lambda o: ptab.at[o + SPAN], lambda d: pt_s.at[d + SPAN], lambda o: pt_r.at[o + SPAN])
    exchange_start(*pt)
    edges(di_ref[...], dw_ref[...], dc_ref[...], (r - SPAN) * m_rows, WIN * m_rows, d_tile, dpos, dwt)
    exchange_recv(*pt)
    b_g = []
    p_rows = kp * p_tile
    for t in range(m_rows // p_tile):
        at = pl.ds(t * p_tile, p_tile)
        messages(
            ptab[...].reshape(-1, width), 0, ppos, pwt, t * p_rows, kp, p_tile, 1, m1.at[0], t * p_tile, agg2.at[0, at]
        )
        g = Gather(
            agg2.at[0, at],
            lambda s, at=at: agg2.at[s + 1, at],
            lambda s, t=t: a2_s.at[s, t],
            lambda s, t=t: a2_r.at[s, t],
        )
        g.start()
        b_g.append(g)
    po_g.forward()
    for g in b_g:
        g.forward()
    po_g.finish()
    for g in b_g:
        g.finish()
    update(lambda j: m1[j], agg2, proc_out, pobuf, mn)

    project(mn, dec_send, dtab)
    dt = (lambda o: dtab.at[o + SPAN], lambda d: dt_s.at[d + SPAN], lambda o: dt_r.at[o + SPAN])
    exchange_start(*dt)
    mesh_next[...] = mn[0]
    exchange_recv(*dt)
    tiles = g_rows // m_rows
    per = kd * m_rows
    out_g = []

    def write(t):
        at = pl.ds(t * m_rows, m_rows)
        acc = grid_state[at, :].astype(F32) + dot(agg3[0, t], wrows(dec_out, 0))
        out_g[t].finish()
        for j in range(1, 4):
            acc = acc + dot(agg3[j, t], wrows(dec_out, j))
        grid_next[at, :] = acc.astype(BF)

    for t in range(tiles):
        messages(
            dtab[...].reshape(-1, width), 0, dpos, dwt, t * per, kd, d_tile, m_rows // d_tile,
            grid_state, t * m_rows, agg3.at[0, t],
        )
        g = Gather(
            agg3.at[0, t],
            lambda s, t=t: agg3.at[s + 1, t],
            lambda s, t=t: a3_s.at[s, t],
            lambda s, t=t: a3_r.at[s, t],
        )
        g.start()
        out_g.append(g)
        if t > 0:
            out_g[t - 1].forward()
    for t in range(tiles):
        if t == tiles - 1:
            out_g[t].forward()
        write(t)

    for g in pending:
        g.drain()
    for w in window:
        exchange_drain(*w)
    for d in OFFSETS:
        @pl.when(inside(d))
        def _(d=d):
            back(d).wait_send()
    exchange_drain(*pt)
    exchange_drain(*dt)


def shards(*args):
    grid_state, mesh_state = args[:2]
    n_region = lax.axis_size("region")
    assert lax.axis_size("chan") == 4
    g_rows, width = grid_state.shape
    m_rows = mesh_state.shape[0]
    full = args[2].shape[0]
    cr = g_rows // CH
    tiles = g_rows // m_rows
    ke, kp, kd = args[8].shape[0], args[11].shape[0], args[14].shape[0]
    args = list(args)
    for i in (10, 13, 16):
        args[i] = args[i].reshape(1, -1)
    dma = pltpu.SemaphoreType.DMA
    V = pltpu.VMEM
    lanes = 128
    scratch = [
        *[V((full, width), BF) for _ in range(5)],
        dma((5,)),
        V((3, CH, cr, width), BF),
        V((3, m_rows, width), BF),
        V((3, full, width), BF),
        V((3, full, width), BF),
        V((WIN, m_rows, width), BF),
        V((WIN, ke, m_rows), jnp.int32),
        V((WIN, ke, m_rows), F32),
        V((WIN, 1, m_rows), jnp.int32),
        V((WIN, m_rows, width), BF),
        V((WIN, m_rows, width), BF),
        V((m_rows, width), F32),
        V((g_rows, width), BF),
        V((WIN, m_rows, width), BF),
        V((WIN, m_rows, width), BF),
        V((WIN, ke * m_rows, lanes), jnp.int16),
        V((WIN, ke * m_rows, lanes), BF),
        V((kp * m_rows, lanes), jnp.int16),
        V((kp * m_rows, lanes), BF),
        V((kd * g_rows, lanes), jnp.int16),
        V((kd * g_rows, lanes), BF),
        V((WIN, ke * m_rows, width), BF),
        V((2048, width), BF),
        V((4, m_rows, width), BF),
        V((4, m_rows, width), BF),
        V((4, tiles, m_rows, width), BF),
        V((4, m_rows, width), BF),
        V((4, m_rows, width), BF),
        dma((3, CH)),
        dma((3, CH)),
        dma((3,)),
        dma((3,)),
        dma((3,)),
        dma((3,)),
        dma((3,)),
        dma((3,)),
        dma((3,)),
        dma((3,)),
        dma((3, 2)),
        dma((3, 2)),
        dma((3, tiles)),
        dma((3, tiles)),
        dma((4, WIN)),
        dma((4, WIN)),
        dma((WIN,)),
        dma((WIN,)),
        dma((WIN,)),
        dma((WIN,)),
        dma((WIN,)),
        dma((WIN,)),
    ]
    return pl.pallas_call(
        functools.partial(kernel, n_region),
        out_shape=(
            jax.ShapeDtypeStruct((g_rows, width), BF),
            jax.ShapeDtypeStruct((m_rows, width), BF),
        ),
        in_specs=[
            pl.BlockSpec(memory_space=pl.ANY if 3 <= i <= 7 else pltpu.VMEM) for i in range(17)
        ],
        out_specs=(pl.BlockSpec(memory_space=pltpu.VMEM),) * 2,
        scratch_shapes=scratch,
        compiler_params=pltpu.CompilerParams(
            collective_id=0, has_side_effects=True, vmem_limit_bytes=56 * 1024 * 1024
        ),
    )(*args)


def solution(mesh):
    placed = (
        P("region", "chan"),
        P("region", "chan"),
        P(None, "chan"),
        P(None, "chan"),
        P(None, "chan"),
        P(None, "chan"),
        P(None, "chan"),
        P(None, "chan"),
        P(None, "region"),
        P(None, "region"),
        P("region"),
        P(None, "region"),
        P(None, "region"),
        P("region"),
        P(None, "region"),
        P(None, "region"),
        P("region"),
    )
    return jax.shard_map(
        shards,
        mesh=mesh,
        in_specs=placed,
        out_specs=(P("region", "chan"), P("region", "chan")),
        check_vma=False,
    )
```
